256 devices in a mesh: ta: 4 (over x), ha: 32 (over z, y_lo, core), ga: 2 (over y_hi).
Axes of the slice: x: 4, y: 4 (y_hi: 2, y_lo: 2; y = y_hi * 2 + y_lo), z: 8, core: 2. Of those that a mesh axis runs over, the one named last changes fastest.
Arguments:
- query_in: bfloat16 [12, 32, 8, 8, 512], P('ta', 'ha', None, None, 'ga'), may hold values from -6 to 6
- key_in: bfloat16 [12, 32, 8, 8, 512], P('ta', 'ha', None, None, 'ga'), may hold values from -6.0625 to 6.0625
- value_in: bfloat16 [12, 32, 8, 8, 512], P('ta', 'ha', None, None, 'ga'), may hold values from -6 to 6
- saved_out: bfloat16 [12, 32, 8, 8, 512], P('ta', 'ha', None, None, 'ga'), may hold values from -6 to 6
- out_grad: bfloat16 [12, 32, 8, 8, 512], P('ta', 'ha', None, None, 'ga'), may hold values from -6 to 6
- window_mask: int32 [2, 4, 8, 27], replicated, may hold values from 0 to 1, as said below
Outputs:
- query_grad: bfloat16 [12, 32, 8, 8, 512], P('ta', 'ha', None, None, 'ga')
- key_grad: bfloat16 [12, 32, 8, 8, 512], P('ta', 'ha', None, None, 'ga')
- value_grad: bfloat16 [12, 32, 8, 8, 512], P('ta', 'ha', None, None, 'ga')
The draws below stay inside these ranges and needn't reach their ends.
Inputs may be any that keep to these rules, and one draw needn't show every extreme that they name: `window_mask`: entry 13 (the tile itself) is 1 for every tile.
All inputs are finite; a program needn't handle non-finite values.
Results may differ from the reference program's by a relative error of at most 0.0058.
Values may be sent and summed in bfloat16 or wider, within the bound.
No kernel may reach another device: no remote copies, remote signals or barrier semaphores. Data moves between devices by JAX's collectives and lax.ppermute only.
A program may use at most 128 MiB of HBM per device.

```python
import jax
import jax.numpy as jnp
from jax import lax

HEAD_DIM = 128
HEADS = 4
TILE_T = 6
TILE_H = 8
TILE_W = 8
FRAMES_DEV = 3
FRAMES = 12
W_TILES = 8
H_TILES = 4
PLANE_TILES = 32
T_TILES = 2
HD = 512
N_TA = 4
N_HA = 32


def draw_query_in(key, part):
    key = jax.random.fold_in(key, 1)
    full_shape = (FRAMES, PLANE_TILES, TILE_H, TILE_W, HEADS * HEAD_DIM)
    values = jnp.clip(jax.random.normal(key, full_shape, jnp.float32), -6.0, 6.0)
    return values.astype(jnp.bfloat16)


def draw_key_in(key, part):
    key = jax.random.fold_in(key, 2)
    full_shape = (FRAMES, PLANE_TILES, TILE_H, TILE_W, HEADS * HEAD_DIM)
    values = jnp.clip(jax.random.normal(key, full_shape, jnp.float32), -6.0, 6.0)
    return values.astype(jnp.bfloat16)


def draw_window_mask(key, part):
    key = jax.random.fold_in(key, 5)
    raw = jax.random.randint(key, (T_TILES, H_TILES, W_TILES, 27), 0, 4)
    centre = jnp.arange(27) == 13
    return jnp.where(centre, 1, jnp.minimum(raw, 1)).astype(jnp.int32)


def level_of(stream_key, extent, cuts, least, largest):
    def one(dim, shards_of):
        heights = jax.random.uniform(jax.random.fold_in(jax.random.fold_in(stream_key, 6), dim), (shards_of,), jnp.float32, least / len(cuts), largest / len(cuts))
        return jnp.repeat(jnp.exp(heights), extent[dim] // shards_of).reshape((-1,) + (1,) * (len(extent) - dim - 1))

    loudness = one(*cuts[0])
    for cut in cuts[1:]:
        loudness = loudness * one(*cut)
    return loudness


def scatter_about(rng, shape, spread, limit, split=(), kind=jnp.bfloat16):
    values = jax.random.normal(rng, shape, jnp.float32) * spread
    if len(split) > 0:
        values = level_of(rng, shape, split, -0.22, 0.18) * values
    return jnp.clip(values, min=-limit, max=limit).astype(kind)


def setup_inputs(seed: int = 0) -> dict:
    key_of = jax.random.split(jax.random.key(seed), 7)
    query_in = draw_query_in(jax.random.fold_in(key_of[6], 71), 0)
    key_in = draw_key_in(jax.random.fold_in(key_of[6], 71), 0)
    value_in = scatter_about(key_of[2], (FRAMES, PLANE_TILES, TILE_H, TILE_W, HD), 1.0, 6.0, ((0, 4), (1, 32), (4, 2)))
    saved_out = scatter_about(key_of[3], (FRAMES, PLANE_TILES, TILE_H, TILE_W, HD), 1.0, 6.0, ((0, 4), (1, 32), (4, 2)))
    out_grad = scatter_about(key_of[4], (FRAMES, PLANE_TILES, TILE_H, TILE_W, HD), 1.0, 6.0, ((0, 4), (1, 32), (4, 2)))
    window_mask = draw_window_mask(jax.random.fold_in(key_of[6], 71), 0)
    return {"query_in": query_in, "key_in": key_in, "value_in": value_in, "saved_out": saved_out, "out_grad": out_grad, "window_mask": window_mask}


def attend(query_rows, key_rows, value_rows, saved_rows, grad_rows, allowed, score_scale):
    f32 = jnp.float32
    scores = jnp.einsum("qhd,khd->hqk", query_rows.astype(f32), key_rows.astype(f32)) * score_scale
    scores = jnp.where(allowed[None, None, :], scores, -jnp.inf)
    row_max = jnp.max(scores, axis=-1, keepdims=True)
    raised = jnp.exp(scores - row_max)
    weights = raised / jnp.sum(raised, axis=-1, keepdims=True)
    weights_low = weights.astype(jnp.bfloat16)
    value_part = jnp.einsum("hqk,qhd->khd", weights_low.astype(f32), grad_rows.astype(f32)).astype(jnp.bfloat16)
    weight_grad = jnp.einsum("qhd,khd->hqk", grad_rows.astype(f32), value_rows.astype(f32))
    row_dot = jnp.einsum("qhd,qhd->hq", grad_rows.astype(f32), saved_rows.astype(f32))
    score_grad = (weights * (weight_grad - row_dot[:, :, None]) * score_scale).astype(jnp.bfloat16)
    query_part = jnp.einsum("hqk,khd->qhd", score_grad.astype(f32), key_rows.astype(f32)).astype(jnp.bfloat16)
    key_part = jnp.einsum("hqk,qhd->khd", score_grad.astype(f32), query_rows.astype(f32)).astype(jnp.bfloat16)
    return query_part, key_part, value_part


def reference(query_in, key_in, value_in, saved_out, out_grad, window_mask):
    score_scale = HEAD_DIM ** -0.5
    grid = (FRAMES, H_TILES, W_TILES, TILE_H, TILE_W, HD)
    pad_spec = ((0, 0), (1, 1), (1, 1), (0, 0), (0, 0), (0, 0))
    key_pad = jnp.pad(key_in.reshape(grid), pad_spec)
    value_pad = jnp.pad(value_in.reshape(grid), pad_spec)
    region = (FRAMES, 3, 3, TILE_H, TILE_W)
    frame_tile = jnp.broadcast_to((jnp.arange(FRAMES, dtype=jnp.int32) // TILE_T).reshape(-1, 1, 1, 1, 1), region).reshape(-1)
    row_step = jnp.broadcast_to((jnp.arange(3, dtype=jnp.int32) - 1).reshape(1, -1, 1, 1, 1), region).reshape(-1)
    col_step = jnp.broadcast_to((jnp.arange(3, dtype=jnp.int32) - 1).reshape(1, 1, -1, 1, 1), region).reshape(-1)
    zero = jnp.zeros((), jnp.int32)
    key_size = (FRAMES, 3, 3, TILE_H, TILE_W, HD)

    def step(carry, block):
        key_sum, value_sum = carry
        time_index = block // N_HA
        plane = block % N_HA
        row_tile = plane // W_TILES
        col_tile = plane % W_TILES
        query_time = (time_index * FRAMES_DEV) // TILE_T
        query_start = (time_index * FRAMES_DEV, plane, zero, zero, zero)
        query_size = (FRAMES_DEV, 1, TILE_H, TILE_W, HD)
        query_rows = lax.dynamic_slice(query_in, query_start, query_size).reshape(-1, HEADS, HEAD_DIM)
        saved_rows = lax.dynamic_slice(saved_out, query_start, query_size).reshape(-1, HEADS, HEAD_DIM)
        grad_rows = lax.dynamic_slice(out_grad, query_start, query_size).reshape(-1, HEADS, HEAD_DIM)
        key_start = (zero, row_tile, col_tile, zero, zero, zero)
        key_rows = lax.dynamic_slice(key_pad, key_start, key_size).reshape(-1, HEADS, HEAD_DIM)
        value_rows = lax.dynamic_slice(value_pad, key_start, key_size).reshape(-1, HEADS, HEAD_DIM)
        window_row = lax.dynamic_slice(window_mask, (query_time, row_tile, col_tile, zero), (1, 1, 1, 27)).reshape(27)
        code = (frame_tile - query_time + 1) * 9 + (row_step + 1) * 3 + (col_step + 1)
        picked = jnp.take(window_row, code.astype(jnp.int32))
        inside = (row_tile + row_step >= 0) & (row_tile + row_step < H_TILES)
        inside = inside & (col_tile + col_step >= 0) & (col_tile + col_step < W_TILES)
        allowed = (picked == 1) & inside
        query_part, key_part, value_part = attend(query_rows, key_rows, value_rows, saved_rows, grad_rows, allowed, score_scale)
        key_sum = lax.dynamic_update_slice(key_sum, lax.dynamic_slice(key_sum, key_start, key_size) + key_part.reshape(key_size).astype(jnp.float32), key_start)
        value_sum = lax.dynamic_update_slice(value_sum, lax.dynamic_slice(value_sum, key_start, key_size) + value_part.reshape(key_size).astype(jnp.float32), key_start)
        return (key_sum, value_sum), query_part.reshape(query_size)

    start_sums = (jnp.zeros(key_pad.shape, jnp.float32), jnp.zeros(key_pad.shape, jnp.float32))
    (key_sum, value_sum), query_blocks = lax.scan(step, start_sums, jnp.arange(N_TA * N_HA, dtype=jnp.int32))
    query_grad = query_blocks.reshape(N_TA, N_HA, FRAMES_DEV, TILE_H, TILE_W, HD).transpose(0, 2, 1, 3, 4, 5).reshape(FRAMES, PLANE_TILES, TILE_H, TILE_W, HD)
    out_shape = (FRAMES, PLANE_TILES, TILE_H, TILE_W, HD)
    key_grad = key_sum[:, 1:H_TILES + 1, 1:W_TILES + 1].reshape(out_shape).astype(jnp.bfloat16)
    value_grad = value_sum[:, 1:H_TILES + 1, 1:W_TILES + 1].reshape(out_shape).astype(jnp.bfloat16)
    return query_grad, key_grad, value_grad
```

```python
import functools

import jax
import jax.numpy as jnp
from jax import lax
from jax.experimental import pallas as pl
from jax.experimental.pallas import tpu as pltpu
from jax.sharding import PartitionSpec as P

HEAD_DIM = 128
TILE_T = 6
CLOSED = 1e30
SCALE = HEAD_DIM ** (-0.5)
SCALE2 = SCALE * 1.4426950408889634
F32 = jnp.float32
BF16 = jnp.bfloat16
NT = (((1,), (1,)), ((), ()))
NN = (((1,), (0,)), ((), ()))
TN = (((0,), (0,)), ((), ()))


def dot(a, b, dims, precision=None):
    return lax.dot_general(a, b, dims, precision=precision, preferred_element_type=F32)


def moved(block, axis, route):
    return lax.ppermute(block, axis, route)


def head_cols(head):
    return pl.ds(head * HEAD_DIM, HEAD_DIM)


def query_columns(own_ref, piece_refs, start, head):
    rows = own_ref.shape[0]
    cols = head_cols(head)
    parts = [own_ref[:, cols]] + [r[pl.ds(start, rows), cols] for r in piece_refs]
    return jnp.concatenate(parts, axis=0)


def stats_kernel(blocks, slots, first, *refs):
    if first:
        bias_ref, own_ref, saved_ref, grad_ref, *refs = refs
        pieces, keys, (out_ref,) = refs[:3], refs[3:-1], refs[-1:]
    else:
        bias_ref, prior_ref, own_ref, *refs = refs
        pieces, keys, (out_ref,) = refs[:3], refs[3:-1], refs[-1:]
    heads = own_ref.shape[1] // HEAD_DIM
    rows = own_ref.shape[0]
    out_ref[...] = jnp.zeros_like(out_ref)
    for head in range(heads):
        query = query_columns(own_ref, pieces, 0, head)
        cols = head_cols(head)
        scores = []
        tops = []
        for (ref, start), slot in zip(blocks, slots):
            s = dot(keys[ref][pl.ds(start, rows), cols], query, NT)
            scores.append(s)
            tops.append(jnp.max(s, axis=0, keepdims=True) * SCALE2 - bias_ref[slot : slot + 1, :])
        top = jnp.maximum(functools.reduce(jnp.maximum, tops), -0.5 * CLOSED)
        if not first:
            top = jnp.maximum(top, prior_ref[head : head + 1, :])
        total = jnp.zeros_like(top)
        for s, slot in zip(scores, slots):
            raised = jnp.exp2(s * SCALE2 - (top + bias_ref[slot : slot + 1, :]))
            total = total + jnp.sum(raised, axis=0, keepdims=True)
        if first:
            product = grad_ref[:, cols].astype(F32) * saved_ref[:, cols].astype(F32)
            ones = jnp.ones((8, HEAD_DIM), F32)
            row_dot = dot(ones, product, NT, lax.Precision.HIGHEST)[:1]
            out_ref[2 * heads + head : 2 * heads + head + 1, 0:rows] = row_dot
        else:
            total = total + prior_ref[heads + head : heads + head + 1, :] * jnp.exp2(
                prior_ref[head : head + 1, :] - top
            )
            out_ref[2 * heads + head : 2 * heads + head + 1, :] = prior_ref[
                2 * heads + head : 2 * heads + head + 1, :
            ]
        out_ref[head : head + 1, :] = top
        out_ref[heads + head : heads + head + 1, :] = total


def rolled(row, shift):
    if shift == 0:
        return row
    width = row.shape[1]
    return jnp.concatenate([row[:, width - shift :], row[:, : width - shift]], axis=1)


def merge_kernel(heads, rows, *refs):
    *stats, out_ref = refs
    tables = [rolled(ref[...], rows * place) for place, ref in enumerate(stats)]
    out_ref[...] = jnp.zeros_like(out_ref)
    top = functools.reduce(jnp.maximum, [t[0:heads] for t in tables])
    total = sum(t[heads : 2 * heads] * jnp.exp2(t[0:heads] - top) for t in tables)
    out_ref[0:heads, :] = top + jnp.log2(total)
    out_ref[heads : 2 * heads, :] = sum(t[2 * heads : 3 * heads] for t in tables)


def grads_kernel(blocks, slots, outs, first, *refs):
    bias_ref, lse_ref, own_q, own_g, p1, p2, p3, *refs = refs
    pieces = (p1, p2, p3)
    n_in = max(b[0] for b in blocks) + 1
    keys, refs = refs[:n_in], refs[n_in:]
    values, refs = refs[:n_in], refs[n_in:]
    if not first:
        prior_ref, *refs = refs
    *part_refs, dq_ref = refs
    heads = own_q.shape[1] // HEAD_DIM
    rows = own_q.shape[0]
    for head in range(heads):
        cols = head_cols(head)
        query = query_columns(own_q, pieces, 0, head)
        grad = query_columns(own_g, pieces, rows, head)
        lse = lse_ref[head : head + 1, :]
        row_dot = lse_ref[heads + head : heads + head + 1, :] * SCALE
        dq = None if first else prior_ref[:, cols]
        for (ref, start), slot, (out, at) in zip(blocks, slots, outs):
            key = keys[ref][pl.ds(start, rows), cols]
            value = values[ref][pl.ds(start, rows), cols]
            s = dot(key, query, NT)
            weights = jnp.exp2(s * SCALE2 - (lse + bias_ref[slot : slot + 1, :]))
            dp = dot(value, grad, NT)
            score_grad = (weights * (dp * SCALE - row_dot)).astype(BF16)
            part = part_refs[out]
            half = part.shape[0] // 2
            part[pl.ds(at, rows), cols] = dot(score_grad, query, NN).astype(part.dtype)
            part[pl.ds(half + at, rows), cols] = dot(weights.astype(BF16), grad, NN).astype(
                part.dtype
            )
            step = dot(score_grad, key, TN)
            dq = step if dq is None else dq + step
        dq_ref[:, cols] = dq


def call(kernel, out_shape, *args):
    many = isinstance(out_shape, (tuple, list))
    vmem = pl.BlockSpec(memory_space=pltpu.VMEM)
    return pl.pallas_call(
        kernel,
        out_shape=out_shape,
        in_specs=[vmem] * len(args),
        out_specs=[vmem] * len(out_shape) if many else vmem,
        compiler_params=pltpu.CompilerParams(vmem_limit_bytes=32 * 1024 * 1024),
    )(*args)


def local(query_in, key_in, value_in, saved_out, out_grad, window_mask):
    frames_dev, _, tile_rows, tile_cols, width = query_in.shape
    rows = frames_dev * tile_rows * tile_cols
    heads = width // HEAD_DIM
    n_ta = lax.axis_size("ta")
    n_ha = lax.axis_size("ha")
    row_tiles, col_tiles = window_mask.shape[1:3]
    me = lax.axis_index("ta")
    plane = lax.axis_index("ha")
    row_tile = plane // col_tiles
    col_tile = plane % col_tiles

    down = [(i, i + col_tiles) for i in range(n_ha - col_tiles)]
    up = [(d, s) for s, d in down]
    right = [(i, i + 1) for i in range(n_ha) if (i + 1) % col_tiles]
    left = [(d, s) for s, d in right]

    q, k, v, o, g = (
        x.reshape(rows, width) for x in (query_in, key_in, value_in, saved_out, out_grad)
    )
    k_up = moved(k, "ha", down)
    k_down = moved(k, "ha", up)
    qg = jnp.concatenate([q, g], axis=0)
    pieces = [
        moved(qg, "ta", [(i, (i + d) % n_ta) for i in range(n_ta)]) for d in range(1, n_ta)
    ]
    k_col = jnp.concatenate([k_up, k, k_down], axis=0)
    k_left = moved(k_col, "ha", right)
    k_right = moved(k_col, "ha", left)
    v_up = moved(v, "ha", down)
    v_down = moved(v, "ha", up)
    v_col = jnp.concatenate([v_up, v, v_down], axis=0)
    v_left = moved(v_col, "ha", right)
    v_right = moved(v_col, "ha", left)

    slot = jnp.arange(16, dtype=jnp.int32)
    row_step = slot // 3 - 1
    col_step = slot % 3 - 1
    inside = (row_tile + row_step >= 0) & (row_tile + row_step < row_tiles)
    inside = inside & (col_tile + col_step >= 0) & (col_tile + col_step < col_tiles) & (slot < 9)
    key_time = me * frames_dev // TILE_T
    owner = (me - jnp.arange(n_ta, dtype=jnp.int32)) % n_ta
    query_time = owner * frames_dev // TILE_T
    windows = lax.dynamic_slice(
        window_mask, (0, row_tile, col_tile, 0), (window_mask.shape[0], 1, 1, 27)
    ).reshape(-1, 27)
    padded = jnp.pad(windows, ((0, 0), (0, 16)))
    table = jnp.zeros((16, n_ta), jnp.int32)
    for t in range(window_mask.shape[0]):
        part = lax.dynamic_slice(padded, (t, (key_time - t + 1) * 9), (1, 16)).reshape(16, 1)
        table = jnp.where(query_time[None, :] == t, part, table)
    bias = jnp.where((table == 1) & inside[:, None], 0.0, CLOSED).astype(F32)
    bias = jnp.repeat(bias, rows, axis=1)

    n_q = n_ta * rows
    stat_shape = jax.ShapeDtypeStruct((8, n_q), F32)
    col_blocks = [(0, 0), (0, rows), (0, 2 * rows)]
    side_blocks = col_blocks + [(1, 0), (1, rows), (1, 2 * rows)]
    mid_slots = (1, 4, 7)
    side_slots = (0, 3, 6, 2, 5, 8)
    stats = call(
        functools.partial(stats_kernel, col_blocks, mid_slots, True),
        stat_shape, bias, q, o, g, *pieces, k_col,
    )
    stats = call(
        functools.partial(stats_kernel, side_blocks, side_slots, False),
        stat_shape, bias, stats, q, *pieces, k_left, k_right,
    )
    others = [
        moved(stats, "ta", [(i, (i + d) % n_ta) for i in range(n_ta)]) for d in range(1, n_ta)
    ]
    lse = call(functools.partial(merge_kernel, heads, rows), stat_shape, stats, *others)
    part_shape = jax.ShapeDtypeStruct((6 * rows, width), BF16)
    mid_shape = jax.ShapeDtypeStruct((6 * rows, width), F32)
    dq_shape = jax.ShapeDtypeStruct((n_q, width), F32)
    col_outs = [(0, 0), (0, rows), (0, 2 * rows)]
    side_outs = col_outs + [(1, 0), (1, rows), (1, 2 * rows)]
    part_left, part_right, dq_side = call(
        functools.partial(grads_kernel, side_blocks, side_slots, side_outs, True),
        (part_shape, part_shape, dq_shape),
        bias, lse, q, g, *pieces, k_left, k_right, v_left, v_right,
    )
    back_left = moved(part_left, "ha", left)
    back_right = moved(part_right, "ha", right)
    part_mid, dq = call(
        functools.partial(grads_kernel, col_blocks, mid_slots, col_outs, False),
        (mid_shape, dq_shape),
        bias, lse, q, g, *pieces, k_col, v_col, dq_side,
    )
    dq_parts = dq.reshape(n_ta, rows, width)
    dq_back = [
        moved(dq_parts[d].astype(BF16), "ta", [(i, (i - d) % n_ta) for i in range(n_ta)])
        for d in range(1, n_ta)
    ]
    total = part_mid + back_left.astype(F32) + back_right.astype(F32)
    total = total.reshape(2, 3, rows, width)
    from_down = moved(total[:, 0].astype(BF16), "ha", up)
    from_up = moved(total[:, 2].astype(BF16), "ha", down)
    whole = (total[:, 1] + from_down.astype(F32) + from_up.astype(F32)).astype(BF16)
    query_grad = (dq_parts[0] + sum(x.astype(F32) for x in dq_back)).astype(BF16)
    shape = query_in.shape
    return query_grad.reshape(shape), whole[0].reshape(shape), whole[1].reshape(shape)


def solution(mesh):
    spec = P("ta", "ha", None, None, "ga")
    return jax.shard_map(
        local,
        mesh=mesh,
        in_specs=(spec,) * 5 + (P(),),
        out_specs=(spec,) * 3,
        check_vma=False,
    )
```

```python
import functools

import jax
import jax.numpy as jnp
from jax import lax
from jax.experimental import pallas as pl
from jax.experimental.pallas import tpu as pltpu
from jax.sharding import PartitionSpec as P

HEAD_DIM = 128
TILE_T = 6
CLOSED = 1e30
SCALE = HEAD_DIM ** (-0.5)
SCALE2 = SCALE * 1.4426950408889634
F32 = jnp.float32
BF16 = jnp.bfloat16
NT = (((1,), (1,)), ((), ()))
NN = (((1,), (0,)), ((), ()))
TN = (((0,), (0,)), ((), ()))


def dot(a, b, dims, precision=None):
    return lax.dot_general(a, b, dims, precision=precision, preferred_element_type=F32)


def head_cols(head):
    return pl.ds(head * HEAD_DIM, HEAD_DIM)


def gathered(piece_refs, half, head):
    rows = piece_refs[0].shape[0] // 2
    return jnp.concatenate(
        [r[pl.ds(half * rows, rows), head_cols(head)] for r in piece_refs], axis=0
    )


def stack_kernel(rows, *refs):
    *parts, out_ref = refs
    for half in range(2):
        for i, ref in enumerate(parts):
            out_ref[pl.ds((3 * half + i) * rows, rows), :] = ref[pl.ds(half * rows, rows), :]


def scores_kernel(position, *refs):
    bias_ref, *refs = refs
    *pieces, kv_ref, weights_ref, stats_ref = refs
    heads = pieces[0].shape[1] // HEAD_DIM
    rows = pieces[0].shape[0] // 2
    stats_ref[...] = jnp.zeros_like(stats_ref)
    for head in range(heads):
        cols = head_cols(head)
        query = gathered(pieces, 0, head)
        scores = []
        tops = []
        for row in range(3):
            key = kv_ref[pl.ds(row * rows, rows), cols]
            at = 3 * position + row
            s = dot(key, query, NT)
            scores.append(s)
            tops.append(jnp.max(s, axis=0, keepdims=True) * SCALE2 - bias_ref[at : at + 1, :])
        top = jnp.maximum(functools.reduce(jnp.maximum, tops), -0.5 * CLOSED)
        total = jnp.zeros_like(top)
        for row, s in enumerate(scores):
            at = 3 * position + row
            raised = jnp.exp2(s * SCALE2 - (top + bias_ref[at : at + 1, :]))
            weights_ref[head, pl.ds(row * rows, rows), :] = raised
            total = total + jnp.sum(raised, axis=0, keepdims=True)
        stats_ref[head : head + 1, :] = top
        stats_ref[heads + head : heads + head + 1, :] = total


def table_kernel(heads, own_o, own_qg, *refs):
    *stats, out_ref = refs
    rows = own_o.shape[0]
    out_ref[...] = jnp.zeros_like(out_ref)
    top = functools.reduce(jnp.maximum, [ref[0:heads, :] for ref in stats])
    total = sum(ref[heads : 2 * heads, :] * jnp.exp2(ref[0:heads, :] - top) for ref in stats)
    out_ref[0:heads, :] = top
    out_ref[heads : 2 * heads, :] = total
    ones = jnp.ones((8, HEAD_DIM), F32)
    for head in range(heads):
        cols = head_cols(head)
        product = own_qg[pl.ds(rows, rows), cols].astype(F32) * own_o[:, cols].astype(F32)
        row_dot = dot(ones, product, NT, lax.Precision.HIGHEST)[:1]
        out_ref[2 * heads + head : 2 * heads + head + 1, 0:rows] = row_dot


def reordered(table, rows, flip):
    if flip == 0:
        return table
    return jnp.concatenate(
        [table[:, (j ^ flip) * rows : ((j ^ flip) + 1) * rows] for j in range(4)], axis=1
    )


def merge_kernel(heads, rows, *refs):
    *tables, out_ref = refs
    tables = [reordered(ref[...], rows, flip) for flip, ref in zip((1, 2, 3, 0), tables)]
    out_ref[...] = jnp.zeros_like(out_ref)
    top = functools.reduce(jnp.maximum, [t[0:heads] for t in tables])
    total = sum(t[heads : 2 * heads] * jnp.exp2(t[0:heads] - top) for t in tables)
    out_ref[0:heads, :] = top + jnp.log2(total)
    out_ref[heads : 2 * heads, :] = sum(t[2 * heads : 3 * heads] for t in tables)


def product_kernel(*refs):
    *pieces, kv_ref, out_ref = refs
    rows = pieces[0].shape[0] // 2
    for head in range(pieces[0].shape[1] // HEAD_DIM):
        cols = head_cols(head)
        grad = gathered(pieces, 1, head)
        for row in range(3):
            value = kv_ref[pl.ds((3 + row) * rows, rows), cols]
            out_ref[head, pl.ds(row * rows, rows), :] = dot(value, grad, NT)


def grads_kernel(first, *refs):
    lse_ref, stats_ref, weights_ref, p0, p1, p2, p3, product_ref, kv_ref, *refs = refs
    pieces = (p0, p1, p2, p3)
    if not first:
        prior_ref, *refs = refs
    out_ref, dq_ref = refs
    heads = p0.shape[1] // HEAD_DIM
    rows = p0.shape[0] // 2
    for head in range(heads):
        cols = head_cols(head)
        query = gathered(pieces, 0, head)
        grad = gathered(pieces, 1, head)
        scale = jnp.exp2(stats_ref[head : head + 1, :] - lse_ref[head : head + 1, :])
        row_dot = lse_ref[heads + head : heads + head + 1, :] * SCALE
        dq = None if first else prior_ref[:, cols]
        for row in range(3):
            place = pl.ds(row * rows, rows)
            weights = weights_ref[head, place, :] * scale
            score_grad = weights * (product_ref[head, place, :] * SCALE - row_dot)
            score_grad = score_grad.astype(BF16)
            out_ref[place, cols] = dot(score_grad, query, NN).astype(out_ref.dtype)
            value_part = dot(weights.astype(BF16), grad, NN).astype(out_ref.dtype)
            out_ref[pl.ds((3 + row) * rows, rows), cols] = value_part
            step = dot(score_grad, kv_ref[place, cols], TN)
            dq = step if dq is None else dq + step
        dq_ref[:, cols] = dq


def add_kernel(x_ref, y_ref, out_ref):
    out_ref[...] = x_ref[...] + y_ref[...].astype(F32)


def column_kernel(rows, mid_ref, a_ref, own_ref, to_a_ref, to_b_ref):
    for half in range(2):
        for row, out in enumerate((own_ref, to_a_ref, to_b_ref)):
            place = pl.ds((3 * half + row) * rows, rows)
            total = mid_ref[place, :] + a_ref[place, :].astype(F32)
            out[pl.ds(half * rows, rows), :] = total.astype(out.dtype)


def query_kernel(own_ref, a_ref, b_ref, c_ref, out_ref):
    total = own_ref[...] + a_ref[...].astype(F32) + b_ref[...].astype(F32)
    out_ref[...] = (total + c_ref[...].astype(F32)).astype(BF16)


def finish_kernel(dq_ref, own_ref, a_ref, b_ref, query_ref, key_ref, value_ref):
    rows = dq_ref.shape[0]
    query_ref[...] = dq_ref[...]
    for half, out in enumerate((key_ref, value_ref)):
        place = pl.ds(half * rows, rows)
        total = own_ref[place, :] + a_ref[place, :].astype(F32) + b_ref[place, :].astype(F32)
        out[...] = total.astype(BF16)


def call(kernel, out_shape, *args):
    many = isinstance(out_shape, (tuple, list))
    vmem = pl.BlockSpec(memory_space=pltpu.VMEM)
    return pl.pallas_call(
        kernel,
        out_shape=out_shape,
        in_specs=[vmem] * len(args),
        out_specs=[vmem] * len(out_shape) if many else vmem,
        compiler_params=pltpu.CompilerParams(vmem_limit_bytes=16 * 1024 * 1024),
        name=getattr(kernel, "func", kernel).__name__[:-7],
        cost_estimate=pl.CostEstimate(flops=0, bytes_accessed=0, transcendentals=0),
    )(*args)


def after(x, *others):
    return lax.optimization_barrier((x, *others))[0]


def local(query_in, key_in, value_in, saved_out, out_grad, window_mask):
    frames_dev, _, tile_rows, tile_cols, width = query_in.shape
    rows = frames_dev * tile_rows * tile_cols
    heads = width // HEAD_DIM
    n_ta = lax.axis_size("ta")
    row_tiles, col_tiles = window_mask.shape[1:3]
    me = lax.axis_index("ta")
    plane = lax.axis_index("ha")
    row_tile = plane // col_tiles
    col_tile = plane % col_tiles

    def pairs(count, first):
        ends = [(i, i + 1) for i in range(first, count - 1, 2)]
        return ends + [(d, s) for s, d in ends]

    def row_swap(x, first, name):
        route = [
            (s * col_tiles + c, d * col_tiles + c)
            for s, d in pairs(row_tiles, first)
            for c in range(col_tiles)
        ]
        with jax.named_scope(name):
            return lax.ppermute(x, "ha", route)

    def col_swap(x, first, name):
        route = [
            (r * col_tiles + s, r * col_tiles + d)
            for s, d in pairs(col_tiles, first)
            for r in range(row_tiles)
        ]
        with jax.named_scope(name):
            return lax.ppermute(x, "ha", route)

    def ta_swap(x, flip, name):
        with jax.named_scope(name):
            return lax.ppermute(x, "ta", [(i, i ^ flip) for i in range(n_ta)])

    q, k, v, o, g = (
        x.reshape(rows, width) for x in (query_in, key_in, value_in, saved_out, out_grad)
    )
    kv = jnp.concatenate([k, v], axis=0)
    kv_b = row_swap(kv, 1, "kv_row_1")
    kv_a = row_swap(kv, 0, "kv_row_0")
    qg = jnp.concatenate([q, g], axis=0)
    swapped = {flip: ta_swap(qg, flip, "query_ta") for flip in (2, 1, 3)}
    pieces = [qg] + [swapped[flip] for flip in (1, 2, 3)]
    stack_shape = jax.ShapeDtypeStruct((6 * rows, width), BF16)
    kv_mid = call(functools.partial(stack_kernel, rows), stack_shape, kv, kv_a, kv_b)
    kv_right = col_swap(kv_mid, 1, "kv_col_1")
    kv_left = col_swap(kv_mid, 0, "kv_col_0")

    place = jnp.arange(16, dtype=jnp.int32)
    row_step = jnp.where(place < 9, place % 3, 0)
    row_step = jnp.where(row_step == 2, -1, row_step) * (1 - 2 * (row_tile % 2))
    col_step = jnp.where(place < 9, place // 3, 0)
    col_step = jnp.where(col_step == 2, -1, col_step) * (1 - 2 * (col_tile % 2))
    inside = (row_tile + row_step >= 0) & (row_tile + row_step < row_tiles)
    inside = inside & (col_tile + col_step >= 0) & (col_tile + col_step < col_tiles) & (place < 9)
    key_time = me * frames_dev // TILE_T
    owner = me ^ jnp.arange(n_ta, dtype=jnp.int32)
    query_time = owner * frames_dev // TILE_T
    windows = lax.dynamic_slice(
        window_mask, (0, row_tile, col_tile, 0), (window_mask.shape[0], 1, 1, 27)
    ).reshape(-1, 27)
    code = (key_time - query_time[None, :] + 1) * 9 + ((row_step + 1) * 3 + col_step + 1)[:, None]
    number = jnp.arange(27, dtype=jnp.int32)
    hit = code[:, :, None] == number
    table = jnp.zeros((16, n_ta), jnp.int32)
    for t in range(window_mask.shape[0]):
        found = jnp.sum(jnp.where(hit, windows[t], 0), axis=-1)
        table = jnp.where(query_time[None, :] == t, found, table)
    bias = jnp.where((table == 1) & inside[:, None], 0.0, CLOSED).astype(F32)
    bias = jnp.repeat(bias, rows, axis=1)

    n_q = n_ta * rows
    stat_shape = jax.ShapeDtypeStruct((8, n_q), F32)
    weight_shape = jax.ShapeDtypeStruct((heads, 3 * rows, n_q), F32)
    dq_shape = jax.ShapeDtypeStruct((n_q, width), F32)

    def scores(position, kv):
        kernel = functools.partial(scores_kernel, position)
        return call(kernel, (weight_shape, stat_shape), bias, *pieces, kv)

    def products(kv):
        return call(product_kernel, weight_shape, *pieces, kv)

    w_mid, s_mid = scores(0, kv_mid)
    w_a, s_a = scores(1, kv_left)
    w_b, s_b = scores(2, kv_right)
    mine = call(functools.partial(table_kernel, heads), stat_shape, o, qg, s_mid, s_a, s_b)
    swapped = {flip: ta_swap(mine, flip, "stats_ta") for flip in (2, 1, 3)}
    others = tuple(swapped[flip] for flip in (1, 2, 3))
    p_mid, p_a, p_b = products(kv_mid), products(kv_left), products(kv_right)
    others = after(others, p_a, p_b, p_mid)
    lse = call(functools.partial(merge_kernel, heads, rows), stat_shape, *others, mine)

    def grads(stats, weights, product, kv, dtype, *prior):
        part = jax.ShapeDtypeStruct((6 * rows, width), dtype)
        kernel = functools.partial(grads_kernel, not prior)
        return call(
            kernel, (part, dq_shape), lse, stats, weights, *pieces, product, kv, *prior
        )

    d_b, dq = grads(s_b, w_b, p_b, kv_right, BF16)
    d_b = col_swap(d_b, 1, "d_col_1")
    d_a, dq = grads(s_a, w_a, p_a, kv_left, BF16, dq)
    d_a = col_swap(d_a, 0, "d_col_0")
    d_mid, dq = grads(s_mid, w_mid, p_mid, kv_mid, F32, dq)
    dq = dq.reshape(n_ta, rows, width)
    dq_parts = [ta_swap(dq[flip].astype(BF16), flip, "dq_ta") for flip in (2, 1, 3)]
    d_mid = call(add_kernel, jax.ShapeDtypeStruct(d_mid.shape, F32), d_mid, d_b)
    own = jax.ShapeDtypeStruct((2 * rows, width), F32)
    sent = jax.ShapeDtypeStruct((2 * rows, width), BF16)
    own, to_a, to_b = call(
        functools.partial(column_kernel, rows), (own, sent, sent), d_mid, d_a
    )
    d_b = row_swap(to_b, 1, "d_row_1")
    d_a = row_swap(to_a, 0, "d_row_0")
    one = jax.ShapeDtypeStruct((rows, width), BF16)
    dq = call(query_kernel, one, dq[0], *dq_parts)
    outs = call(finish_kernel, (one, one, one), dq, own, d_a, d_b)
    return tuple(x.reshape(query_in.shape) for x in outs)


def solution(mesh):
    spec = P("ta", "ha", None, None, "ga")
    return jax.shard_map(
        local,
        mesh=mesh,
        in_specs=(spec,) * 5 + (P(),),
        out_specs=(spec,) * 3,
        check_vma=False,
    )
```

```python
import functools

import jax
import jax.numpy as jnp
from jax import lax
from jax.experimental import pallas as pl
from jax.experimental.pallas import tpu as pltpu
from jax.sharding import PartitionSpec as P

HEAD_DIM = 128
TILE_T = 6
CLOSED = 1e30
SCALE = HEAD_DIM ** (-0.5)
SCALE2 = SCALE * 1.4426950408889634
F32 = jnp.float32
BF16 = jnp.bfloat16
NT = (((1,), (1,)), ((), ()))
NN = (((1,), (0,)), ((), ()))
TN = (((0,), (0,)), ((), ()))


def dot(a, b, dims, precision=None):
    return lax.dot_general(a, b, dims, precision=precision, preferred_element_type=F32)


def head_cols(head):
    return pl.ds(head * HEAD_DIM, HEAD_DIM)


def gathered(piece_refs, half, head):
    rows = piece_refs[0].shape[0] // 2
    return jnp.concatenate(
        [r[pl.ds(half * rows, rows), head_cols(head)] for r in piece_refs], axis=0
    )


def stack_kernel(rows, *refs):
    *parts, out_ref = refs
    for half in range(2):
        for i, ref in enumerate(parts):
            out_ref[pl.ds((3 * half + i) * rows, rows), :] = ref[pl.ds(half * rows, rows), :]


def scores_kernel(position, *refs):
    bias_ref, *refs = refs
    *pieces, kv_ref, weights_ref, stats_ref = refs
    if position == 0:
        saved_ref, *pieces = pieces
    heads = pieces[0].shape[1] // HEAD_DIM
    rows = pieces[0].shape[0] // 2
    stats_ref[...] = jnp.zeros_like(stats_ref)
    for head in range(heads):
        cols = head_cols(head)
        query = gathered(pieces, 0, head)
        if position == 0:
            product = pieces[0][pl.ds(rows, rows), cols].astype(F32)
            product = product * saved_ref[:, cols].astype(F32)
            ones = jnp.ones((8, HEAD_DIM), F32)
            row_dot = dot(ones, product, NT, lax.Precision.HIGHEST)[:1]
            stats_ref[2 * heads + head : 2 * heads + head + 1, 0:rows] = row_dot
        scores = []
        tops = []
        for row in range(3):
            key = kv_ref[pl.ds(row * rows, rows), cols]
            at = 3 * position + row
            s = dot(key, query, NT)
            scores.append(s)
            tops.append(jnp.max(s, axis=0, keepdims=True) * SCALE2 - bias_ref[at : at + 1, :])
        top = jnp.maximum(functools.reduce(jnp.maximum, tops), -0.5 * CLOSED)
        total = jnp.zeros_like(top)
        for row, s in enumerate(scores):
            at = 3 * position + row
            raised = jnp.exp2(s * SCALE2 - (top + bias_ref[at : at + 1, :]))
            weights_ref[head, pl.ds(row * rows, rows), :] = raised
            total = total + jnp.sum(raised, axis=0, keepdims=True)
        stats_ref[head : head + 1, :] = top
        stats_ref[heads + head : heads + head + 1, :] = total


def table_kernel(heads, *refs):
    *stats, out_ref = refs
    out_ref[...] = stats[0][...]
    top = functools.reduce(jnp.maximum, [ref[0:heads, :] for ref in stats])
    total = sum(ref[heads : 2 * heads, :] * jnp.exp2(ref[0:heads, :] - top) for ref in stats)
    out_ref[0:heads, :] = top
    out_ref[heads : 2 * heads, :] = total


def reordered(table, rows, flip):
    if flip == 0:
        return table
    return jnp.concatenate(
        [table[:, (j ^ flip) * rows : ((j ^ flip) + 1) * rows] for j in range(4)], axis=1
    )


def merge_kernel(heads, rows, *refs):
    *tables, out_ref = refs
    tables = [reordered(ref[...], rows, flip) for flip, ref in zip((1, 2, 3, 0), tables)]
    out_ref[...] = jnp.zeros_like(out_ref)
    top = functools.reduce(jnp.maximum, [t[0:heads] for t in tables])
    total = sum(t[heads : 2 * heads] * jnp.exp2(t[0:heads] - top) for t in tables)
    out_ref[0:heads, :] = top + jnp.log2(total)
    out_ref[heads : 2 * heads, :] = sum(t[2 * heads : 3 * heads] for t in tables)


def product_kernel(*refs):
    *pieces, kv_ref, out_ref = refs
    rows = pieces[0].shape[0] // 2
    for head in range(pieces[0].shape[1] // HEAD_DIM):
        cols = head_cols(head)
        grad = gathered(pieces, 1, head)
        for row in range(3):
            value = kv_ref[pl.ds((3 + row) * rows, rows), cols]
            out_ref[head, pl.ds(row * rows, rows), :] = dot(value, grad, NT)


def grads_kernel(stage, *refs):
    lse_ref, stats_ref, weights_ref, p0, p1, p2, p3, product_ref, kv_ref, *refs = refs
    pieces = (p0, p1, p2, p3)
    if stage == 0:
        out_ref, kept_ref = refs
    elif stage == 1:
        kept_ref, kept_kv_ref, out_ref, dq_ref = refs
    else:
        prior_ref, out_ref, dq_ref = refs
    heads = p0.shape[1] // HEAD_DIM
    rows = p0.shape[0] // 2
    for head in range(heads):
        cols = head_cols(head)
        query = gathered(pieces, 0, head)
        grad = gathered(pieces, 1, head)
        scale = jnp.exp2(stats_ref[head : head + 1, :] - lse_ref[head : head + 1, :])
        row_dot = lse_ref[heads + head : heads + head + 1, :] * SCALE
        if stage == 1:
            whole = pl.ds(0, 3 * rows)
            dq = dot(kept_ref[head], kept_kv_ref[whole, cols], TN)
        elif stage == 2:
            dq = prior_ref[:, cols]
        for row in range(3):
            place = pl.ds(row * rows, rows)
            weights = weights_ref[head, place, :] * scale
            score_grad = weights * (product_ref[head, place, :] * SCALE - row_dot)
            score_grad = score_grad.astype(BF16)
            out_ref[place, cols] = dot(score_grad, query, NN).astype(out_ref.dtype)
            value_part = dot(weights.astype(BF16), grad, NN).astype(out_ref.dtype)
            out_ref[pl.ds((3 + row) * rows, rows), cols] = value_part
            if stage == 0:
                kept_ref[head, place, :] = score_grad
            else:
                dq = dq + dot(score_grad, kv_ref[place, cols], TN)
        if stage:
            dq_ref[:, cols] = dq


def add_kernel(x_ref, y_ref, out_ref):
    out_ref[...] = x_ref[...] + y_ref[...].astype(F32)


def column_kernel(rows, mid_ref, a_ref, own_ref, to_a_ref, to_b_ref):
    for half in range(2):
        for row, out in enumerate((own_ref, to_a_ref, to_b_ref)):
            place = pl.ds((3 * half + row) * rows, rows)
            total = mid_ref[place, :] + a_ref[place, :].astype(F32)
            out[pl.ds(half * rows, rows), :] = total.astype(out.dtype)


def query_kernel(own_ref, a_ref, b_ref, c_ref, out_ref):
    total = own_ref[...] + a_ref[...].astype(F32) + b_ref[...].astype(F32)
    out_ref[...] = (total + c_ref[...].astype(F32)).astype(BF16)


def finish_kernel(dq_ref, own_ref, a_ref, b_ref, query_ref, key_ref, value_ref):
    rows = dq_ref.shape[0]
    query_ref[...] = dq_ref[...]
    for half, out in enumerate((key_ref, value_ref)):
        place = pl.ds(half * rows, rows)
        total = own_ref[place, :] + a_ref[place, :].astype(F32) + b_ref[place, :].astype(F32)
        out[...] = total.astype(BF16)


def call(kernel, out_shape, *args):
    many = isinstance(out_shape, (tuple, list))
    vmem = pl.BlockSpec(memory_space=pltpu.VMEM)
    return pl.pallas_call(
        kernel,
        out_shape=out_shape,
        in_specs=[vmem] * len(args),
        out_specs=[vmem] * len(out_shape) if many else vmem,
        compiler_params=pltpu.CompilerParams(vmem_limit_bytes=16 * 1024 * 1024),
        name=getattr(kernel, "func", kernel).__name__[:-7],
        cost_estimate=pl.CostEstimate(flops=0, bytes_accessed=0, transcendentals=0),
    )(*args)


def after(x, *others):
    return lax.optimization_barrier((x, *others))[0]


def local(query_in, key_in, value_in, saved_out, out_grad, window_mask):
    frames_dev, _, tile_rows, tile_cols, width = query_in.shape
    rows = frames_dev * tile_rows * tile_cols
    heads = width // HEAD_DIM
    n_ta = lax.axis_size("ta")
    row_tiles, col_tiles = window_mask.shape[1:3]
    me = lax.axis_index("ta")
    plane = lax.axis_index("ha")
    row_tile = plane // col_tiles
    col_tile = plane % col_tiles

    def pairs(count, first):
        ends = [(i, i + 1) for i in range(first, count - 1, 2)]
        return ends + [(d, s) for s, d in ends]

    def row_swap(x, first, name):
        route = [
            (s * col_tiles + c, d * col_tiles + c)
            for s, d in pairs(row_tiles, first)
            for c in range(col_tiles)
        ]
        with jax.named_scope(name):
            return lax.ppermute(x, "ha", route)

    def col_swap(x, first, name):
        route = [
            (r * col_tiles + s, r * col_tiles + d)
            for s, d in pairs(col_tiles, first)
            for r in range(row_tiles)
        ]
        with jax.named_scope(name):
            return lax.ppermute(x, "ha", route)

    def ta_swap(x, flip, name):
        with jax.named_scope(name):
            return lax.ppermute(x, "ta", [(i, i ^ flip) for i in range(n_ta)])

    q, k, v, o, g = (
        x.reshape(rows, width) for x in (query_in, key_in, value_in, saved_out, out_grad)
    )
    kv = jnp.concatenate([k, v], axis=0)
    kv_b = row_swap(kv, 1, "kv_row_1")
    kv_a = row_swap(kv, 0, "kv_row_0")
    qg = jnp.concatenate([q, g], axis=0)
    swapped = {flip: ta_swap(qg, flip, "query_ta") for flip in (2, 1, 3)}
    pieces = [qg] + [swapped[flip] for flip in (1, 2, 3)]
    stack_shape = jax.ShapeDtypeStruct((6 * rows, width), BF16)
    kv_mid = call(functools.partial(stack_kernel, rows), stack_shape, kv, kv_a, kv_b)
    kv_right = col_swap(kv_mid, 1, "kv_col_1")
    kv_left = col_swap(kv_mid, 0, "kv_col_0")

    place = jnp.arange(16, dtype=jnp.int32)
    row_step = jnp.where(place < 9, place % 3, 0)
    row_step = jnp.where(row_step == 2, -1, row_step) * (1 - 2 * (row_tile % 2))
    col_step = jnp.where(place < 9, place // 3, 0)
    col_step = jnp.where(col_step == 2, -1, col_step) * (1 - 2 * (col_tile % 2))
    inside = (row_tile + row_step >= 0) & (row_tile + row_step < row_tiles)
    inside = inside & (col_tile + col_step >= 0) & (col_tile + col_step < col_tiles) & (place < 9)
    key_time = me * frames_dev // TILE_T
    owner = me ^ jnp.arange(n_ta, dtype=jnp.int32)
    query_time = owner * frames_dev // TILE_T
    windows = lax.dynamic_slice(
        window_mask, (0, row_tile, col_tile, 0), (window_mask.shape[0], 1, 1, 27)
    ).reshape(-1, 27)
    code = (key_time - query_time[None, :] + 1) * 9 + ((row_step + 1) * 3 + col_step + 1)[:, None]
    number = jnp.arange(27, dtype=jnp.int32)
    hit = code[:, :, None] == number
    table = jnp.zeros((16, n_ta), jnp.int32)
    for t in range(window_mask.shape[0]):
        found = jnp.sum(jnp.where(hit, windows[t], 0), axis=-1)
        table = jnp.where(query_time[None, :] == t, found, table)
    bias = jnp.where((table == 1) & inside[:, None], 0.0, CLOSED).astype(F32)
    bias = jnp.repeat(bias, rows, axis=1)

    n_q = n_ta * rows
    stat_shape = jax.ShapeDtypeStruct((8, n_q), F32)
    weight_shape = jax.ShapeDtypeStruct((heads, 3 * rows, n_q), F32)
    dq_shape = jax.ShapeDtypeStruct((n_q, width), F32)

    def scores(position, kv):
        kernel = functools.partial(scores_kernel, position)
        first = (o,) if position == 0 else ()
        return call(kernel, (weight_shape, stat_shape), bias, *first, *pieces, kv)

    def products(kv):
        return call(product_kernel, weight_shape, *pieces, kv)

    w_mid, s_mid = scores(0, kv_mid)
    w_a, s_a = scores(1, kv_left)
    w_b, s_b = scores(2, kv_right)
    mine = call(functools.partial(table_kernel, heads), stat_shape, s_mid, s_a, s_b)
    swapped = {flip: ta_swap(mine, flip, "stats_ta") for flip in (2, 1, 3)}
    others = tuple(swapped[flip] for flip in (1, 2, 3))
    p_mid, p_a, p_b = products(kv_mid), products(kv_left), products(kv_right)
    others = after(others, p_a, p_b, p_mid)
    lse = call(functools.partial(merge_kernel, heads, rows), stat_shape, *others, mine)

    def grads(stage, stats, weights, product, kv, dtype, *prior):
        part = jax.ShapeDtypeStruct((6 * rows, width), dtype)
        kept = jax.ShapeDtypeStruct(weight_shape.shape, BF16)
        return call(
            functools.partial(grads_kernel, stage),
            (part, dq_shape if stage else kept),
            lse, stats, weights, *pieces, product, kv, *prior,
        )

    d_b, kept = grads(0, s_b, w_b, p_b, kv_right, BF16)
    d_b = col_swap(d_b, 1, "d_col_1")
    d_a, dq = grads(1, s_a, w_a, p_a, kv_left, BF16, kept, kv_right)
    d_a = col_swap(d_a, 0, "d_col_0")
    d_mid, dq = grads(2, s_mid, w_mid, p_mid, kv_mid, F32, dq)
    dq = dq.reshape(n_ta, rows, width)
    dq_parts = [ta_swap(dq[flip].astype(BF16), flip, "dq_ta") for flip in (2, 1, 3)]
    d_mid = call(add_kernel, jax.ShapeDtypeStruct(d_mid.shape, F32), d_mid, d_b)
    own = jax.ShapeDtypeStruct((2 * rows, width), F32)
    sent = jax.ShapeDtypeStruct((2 * rows, width), BF16)
    own, to_a, to_b = call(
        functools.partial(column_kernel, rows), (own, sent, sent), d_mid, d_a
    )
    d_b = row_swap(to_b, 1, "d_row_1")
    d_a = row_swap(to_a, 0, "d_row_0")
    one = jax.ShapeDtypeStruct((rows, width), BF16)
    dq = call(query_kernel, one, dq[0], *dq_parts)
    outs = call(finish_kernel, (one, one, one), dq, own, d_a, d_b)
    return tuple(x.reshape(query_in.shape) for x in outs)


def solution(mesh):
    spec = P("ta", "ha", None, None, "ga")
    return jax.shard_map(
        local,
        mesh=mesh,
        in_specs=(spec,) * 5 + (P(),),
        out_specs=(spec,) * 3,
        check_vma=False,
    )
```

```python
import functools

import jax
import jax.numpy as jnp
from jax import lax
from jax.experimental import pallas as pl
from jax.experimental.pallas import tpu as pltpu
from jax.sharding import PartitionSpec as P

HEAD_DIM = 128
TILE_T = 6
CLOSED = 1e30
SCALE = HEAD_DIM ** (-0.5)
SCALE2 = SCALE * 1.4426950408889634
F32 = jnp.float32
BF16 = jnp.bfloat16
NT = (((1,), (1,)), ((), ()))
NN = (((1,), (0,)), ((), ()))
TN = (((0,), (0,)), ((), ()))


def dot(a, b, dims, precision=None):
    return lax.dot_general(a, b, dims, precision=precision, preferred_element_type=F32)


def head_cols(head):
    return pl.ds(head * HEAD_DIM, HEAD_DIM)


def gathered(piece_refs, half, head):
    rows = piece_refs[0].shape[0] // 2
    return jnp.concatenate(
        [r[pl.ds(half * rows, rows), head_cols(head)] for r in piece_refs], axis=0
    )


def stack_kernel(rows, *refs):
    *parts, out_ref = refs
    for half in range(2):
        for i, ref in enumerate(parts):
            out_ref[pl.ds((3 * half + i) * rows, rows), :] = ref[pl.ds(half * rows, rows), :]


def scores_kernel(position, *refs):
    bias_ref, *refs = refs
    *pieces, kv_ref, weights_ref, stats_ref = refs
    if position == 0:
        saved_ref, *pieces = pieces
    heads = pieces[0].shape[1] // HEAD_DIM
    rows = pieces[0].shape[0] // 2
    stats_ref[...] = jnp.zeros_like(stats_ref)
    for head in range(heads):
        cols = head_cols(head)
        query = gathered(pieces, 0, head)
        if position == 0:
            product = pieces[0][pl.ds(rows, rows), cols].astype(F32)
            product = product * saved_ref[:, cols].astype(F32)
            ones = jnp.ones((8, HEAD_DIM), F32)
            row_dot = dot(ones, product, NT, lax.Precision.HIGHEST)[:1]
            stats_ref[2 * heads + head : 2 * heads + head + 1, 0:rows] = row_dot
        scores = []
        tops = []
        for row in range(3):
            key = kv_ref[pl.ds(row * rows, rows), cols]
            at = 3 * position + row
            s = dot(key, query, NT)
            scores.append(s)
            tops.append(jnp.max(s, axis=0, keepdims=True) * SCALE2 - bias_ref[at : at + 1, :])
        top = jnp.maximum(functools.reduce(jnp.maximum, tops), -0.5 * CLOSED)
        total = jnp.zeros_like(top)
        for row, s in enumerate(scores):
            at = 3 * position + row
            raised = jnp.exp2(s * SCALE2 - (top + bias_ref[at : at + 1, :]))
            weights_ref[head, pl.ds(row * rows, rows), :] = raised
            total = total + jnp.sum(raised, axis=0, keepdims=True)
        stats_ref[head : head + 1, :] = top
        stats_ref[heads + head : heads + head + 1, :] = total


def table_kernel(heads, *refs):
    *stats, out_ref = refs
    out_ref[...] = stats[0][...]
    top = functools.reduce(jnp.maximum, [ref[0:heads, :] for ref in stats])
    total = sum(ref[heads : 2 * heads, :] * jnp.exp2(ref[0:heads, :] - top) for ref in stats)
    out_ref[0:heads, :] = top
    out_ref[heads : 2 * heads, :] = total


def reordered(table, rows, flip):
    if flip == 0:
        return table
    return jnp.concatenate(
        [table[:, (j ^ flip) * rows : ((j ^ flip) + 1) * rows] for j in range(4)], axis=1
    )


def merge_kernel(heads, rows, *refs):
    *tables, out_ref = refs
    tables = [reordered(ref[...], rows, flip) for flip, ref in zip((1, 3, 2, 0), tables)]
    out_ref[...] = jnp.zeros_like(out_ref)
    top = functools.reduce(jnp.maximum, [t[0:heads] for t in tables])
    total = sum(t[heads : 2 * heads] * jnp.exp2(t[0:heads] - top) for t in tables)
    out_ref[0:heads, :] = top + jnp.log2(total)
    out_ref[heads : 2 * heads, :] = sum(t[2 * heads : 3 * heads] for t in tables)


def product_kernel(*refs):
    *pieces, kv_ref, out_ref = refs
    rows = pieces[0].shape[0] // 2
    for head in range(pieces[0].shape[1] // HEAD_DIM):
        cols = head_cols(head)
        grad = gathered(pieces, 1, head)
        for row in range(3):
            value = kv_ref[pl.ds((3 + row) * rows, rows), cols]
            out_ref[head, pl.ds(row * rows, rows), :] = dot(value, grad, NT)


def grads_kernel(stage, *refs):
    lse_ref, stats_ref, weights_ref, p0, p1, p2, p3, product_ref, kv_ref, *refs = refs
    pieces = (p0, p1, p2, p3)
    if stage == 0:
        out_ref, kept_ref = refs
    elif stage == 1:
        kept_ref, kept_kv_ref, out_ref, dq_ref = refs
    else:
        prior_ref, out_ref, dq_ref = refs
    heads = p0.shape[1] // HEAD_DIM
    rows = p0.shape[0] // 2
    for head in range(heads):
        cols = head_cols(head)
        query = gathered(pieces, 0, head)
        grad = gathered(pieces, 1, head)
        scale = jnp.exp2(stats_ref[head : head + 1, :] - lse_ref[head : head + 1, :])
        row_dot = lse_ref[heads + head : heads + head + 1, :] * SCALE
        if stage == 1:
            whole = pl.ds(0, 3 * rows)
            dq = dot(kept_ref[head], kept_kv_ref[whole, cols], TN)
        elif stage == 2:
            dq = prior_ref[:, cols]
        for row in range(3):
            place = pl.ds(row * rows, rows)
            weights = weights_ref[head, place, :] * scale
            score_grad = weights * (product_ref[head, place, :] * SCALE - row_dot)
            score_grad = score_grad.astype(BF16)
            out_ref[place, cols] = dot(score_grad, query, NN).astype(out_ref.dtype)
            value_part = dot(weights.astype(BF16), grad, NN).astype(out_ref.dtype)
            out_ref[pl.ds((3 + row) * rows, rows), cols] = value_part
            if stage == 0:
                kept_ref[head, place, :] = score_grad
            else:
                dq = dq + dot(score_grad, kv_ref[place, cols], TN)
        if stage:
            dq_ref[:, cols] = dq


def add_kernel(x_ref, y_ref, out_ref):
    out_ref[...] = x_ref[...] + y_ref[...].astype(F32)


def column_kernel(rows, mid_ref, a_ref, own_ref, to_a_ref, to_b_ref):
    for half in range(2):
        for row, out in enumerate((own_ref, to_a_ref, to_b_ref)):
            place = pl.ds((3 * half + row) * rows, rows)
            total = mid_ref[place, :] + a_ref[place, :].astype(F32)
            out[pl.ds(half * rows, rows), :] = total.astype(out.dtype)


def query_kernel(own_ref, a_ref, b_ref, c_ref, out_ref):
    total = own_ref[...] + a_ref[...].astype(F32) + b_ref[...].astype(F32)
    out_ref[...] = (total + c_ref[...].astype(F32)).astype(BF16)


def finish_kernel(dq_ref, own_ref, a_ref, b_ref, query_ref, key_ref, value_ref):
    rows = dq_ref.shape[0]
    query_ref[...] = dq_ref[...]
    for half, out in enumerate((key_ref, value_ref)):
        place = pl.ds(half * rows, rows)
        total = own_ref[place, :] + a_ref[place, :].astype(F32) + b_ref[place, :].astype(F32)
        out[...] = total.astype(BF16)


def call(kernel, out_shape, *args):
    many = isinstance(out_shape, (tuple, list))
    vmem = pl.BlockSpec(memory_space=pltpu.VMEM)
    return pl.pallas_call(
        kernel,
        out_shape=out_shape,
        in_specs=[vmem] * len(args),
        out_specs=[vmem] * len(out_shape) if many else vmem,
        compiler_params=pltpu.CompilerParams(vmem_limit_bytes=16 * 1024 * 1024),
        name=getattr(kernel, "func", kernel).__name__[:-7],
        cost_estimate=pl.CostEstimate(flops=0, bytes_accessed=0, transcendentals=0),
    )(*args)


def after(x, *others):
    return lax.optimization_barrier((x, *others))[0]


def local(query_in, key_in, value_in, saved_out, out_grad, window_mask):
    frames_dev, _, tile_rows, tile_cols, width = query_in.shape
    rows = frames_dev * tile_rows * tile_cols
    heads = width // HEAD_DIM
    n_ta = lax.axis_size("ta")
    row_tiles, col_tiles = window_mask.shape[1:3]
    me = lax.axis_index("ta")
    plane = lax.axis_index("ha")
    row_tile = plane // col_tiles
    col_tile = plane % col_tiles

    def pairs(count, first):
        ends = [(i, i + 1) for i in range(first, count - 1, 2)]
        return ends + [(d, s) for s, d in ends]

    def row_swap(x, first, name):
        route = [
            (s * col_tiles + c, d * col_tiles + c)
            for s, d in pairs(row_tiles, first)
            for c in range(col_tiles)
        ]
        with jax.named_scope(name):
            return lax.ppermute(x, "ha", route)

    def col_swap(x, first, name):
        route = [
            (r * col_tiles + s, r * col_tiles + d)
            for s, d in pairs(col_tiles, first)
            for r in range(row_tiles)
        ]
        with jax.named_scope(name):
            return lax.ppermute(x, "ha", route)

    def ta_swap(x, flip, name):
        with jax.named_scope(name):
            return lax.ppermute(x, "ta", [(i, i ^ flip) for i in range(n_ta)])

    q, k, v, o, g = (
        x.reshape(rows, width) for x in (query_in, key_in, value_in, saved_out, out_grad)
    )
    kv = jnp.concatenate([k, v], axis=0)
    kv_b = row_swap(kv, 1, "kv_row_1")
    kv_a = row_swap(kv, 0, "kv_row_0")
    qg = jnp.concatenate([q, g], axis=0)
    swapped = {flip: ta_swap(qg, flip, "query_ta") for flip in (2, 1, 3)}
    pieces = [qg] + [swapped[flip] for flip in (1, 2, 3)]
    stack_shape = jax.ShapeDtypeStruct((6 * rows, width), BF16)
    kv_mid = call(functools.partial(stack_kernel, rows), stack_shape, kv, kv_a, kv_b)
    kv_right = col_swap(kv_mid, 1, "kv_col_1")
    kv_left = col_swap(kv_mid, 0, "kv_col_0")

    place = jnp.arange(16, dtype=jnp.int32)
    row_step = jnp.where(place < 9, place % 3, 0)
    row_step = jnp.where(row_step == 2, -1, row_step) * (1 - 2 * (row_tile % 2))
    col_step = jnp.where(place < 9, place // 3, 0)
    col_step = jnp.where(col_step == 2, -1, col_step) * (1 - 2 * (col_tile % 2))
    inside = (row_tile + row_step >= 0) & (row_tile + row_step < row_tiles)
    inside = inside & (col_tile + col_step >= 0) & (col_tile + col_step < col_tiles) & (place < 9)
    key_time = me * frames_dev // TILE_T
    owner = me ^ jnp.arange(n_ta, dtype=jnp.int32)
    query_time = owner * frames_dev // TILE_T
    windows = lax.dynamic_slice(
        window_mask, (0, row_tile, col_tile, 0), (window_mask.shape[0], 1, 1, 27)
    ).reshape(-1, 27)
    code = (key_time - query_time[None, :] + 1) * 9 + ((row_step + 1) * 3 + col_step + 1)[:, None]
    number = jnp.arange(27, dtype=jnp.int32)
    hit = code[:, :, None] == number
    table = jnp.zeros((16, n_ta), jnp.int32)
    for t in range(window_mask.shape[0]):
        found = jnp.sum(jnp.where(hit, windows[t], 0), axis=-1)
        table = jnp.where(query_time[None, :] == t, found, table)
    bias = jnp.where((table == 1) & inside[:, None], 0.0, CLOSED).astype(F32)
    bias = jnp.repeat(bias, rows, axis=1)

    n_q = n_ta * rows
    stat_shape = jax.ShapeDtypeStruct((8, n_q), F32)
    weight_shape = jax.ShapeDtypeStruct((heads, 3 * rows, n_q), F32)
    dq_shape = jax.ShapeDtypeStruct((n_q, width), F32)

    def scores(position, kv):
        kernel = functools.partial(scores_kernel, position)
        first = (o,) if position == 0 else ()
        return call(kernel, (weight_shape, stat_shape), bias, *first, *pieces, kv)

    def products(kv):
        return call(product_kernel, weight_shape, *pieces, kv)

    w_mid, s_mid = scores(0, kv_mid)
    w_a, s_a = scores(1, kv_left)
    w_b, s_b = scores(2, kv_right)
    mine = call(functools.partial(table_kernel, heads), stat_shape, s_mid, s_a, s_b)
    swapped = {flip: ta_swap(mine, flip, "stats_ta") for flip in (2, 1, 3)}
    others = tuple(swapped[flip] for flip in (1, 3, 2))
    p_mid, p_a, p_b = products(kv_mid), products(kv_left), products(kv_right)
    others = after(others, p_a, p_b, p_mid)
    lse = call(functools.partial(merge_kernel, heads, rows), stat_shape, *others, mine)

    def grads(stage, stats, weights, product, kv, dtype, *prior):
        part = jax.ShapeDtypeStruct((6 * rows, width), dtype)
        kept = jax.ShapeDtypeStruct(weight_shape.shape, BF16)
        return call(
            functools.partial(grads_kernel, stage),
            (part, dq_shape if stage else kept),
            lse, stats, weights, *pieces, product, kv, *prior,
        )

    d_b, kept = grads(0, s_b, w_b, p_b, kv_right, BF16)
    d_b = col_swap(d_b, 1, "d_col_1")
    d_a, dq = grads(1, s_a, w_a, p_a, kv_left, BF16, kept, kv_right)
    d_a = col_swap(d_a, 0, "d_col_0")
    d_mid, dq = grads(2, s_mid, w_mid, p_mid, kv_mid, F32, dq)
    dq = dq.reshape(n_ta, rows, width)
    dq_parts = [ta_swap(dq[flip].astype(BF16), flip, "dq_ta") for flip in (1, 3, 2)]
    d_mid = call(add_kernel, jax.ShapeDtypeStruct(d_mid.shape, F32), d_mid, d_b)
    own = jax.ShapeDtypeStruct((2 * rows, width), F32)
    sent = jax.ShapeDtypeStruct((2 * rows, width), BF16)
    own, to_a, to_b = call(
        functools.partial(column_kernel, rows), (own, sent, sent), d_mid, d_a
    )
    d_b = row_swap(to_b, 1, "d_row_1")
    d_a = row_swap(to_a, 0, "d_row_0")
    one = jax.ShapeDtypeStruct((rows, width), BF16)
    dq = call(query_kernel, one, dq[0], *dq_parts)
    outs = call(finish_kernel, (one, one, one), dq, own, d_a, d_b)
    return tuple(x.reshape(query_in.shape) for x in outs)


def solution(mesh):
    spec = P("ta", "ha", None, None, "ga")
    return jax.shard_map(
        local,
        mesh=mesh,
        in_specs=(spec,) * 5 + (P(),),
        out_specs=(spec,) * 3,
        check_vma=False,
    )
```

```python
import functools

import jax
import jax.numpy as jnp
from jax import lax
from jax.experimental import pallas as pl
from jax.experimental.pallas import tpu as pltpu
from jax.sharding import PartitionSpec as P

HEAD_DIM = 128
TILE_T = 6
CLOSED = 1e30
SCALE = HEAD_DIM ** (-0.5)
SCALE2 = SCALE * 1.4426950408889634
F32 = jnp.float32
BF16 = jnp.bfloat16
NT = (((1,), (1,)), ((), ()))
NN = (((1,), (0,)), ((), ()))
TN = (((0,), (0,)), ((), ()))


def dot(a, b, dims, precision=None):
    return lax.dot_general(a, b, dims, precision=precision, preferred_element_type=F32)


def head_cols(head):
    return pl.ds(head * HEAD_DIM, HEAD_DIM)


def gathered(piece_refs, half, head):
    rows = piece_refs[0].shape[0] // 2
    return jnp.concatenate(
        [r[pl.ds(half * rows, rows), head_cols(head)] for r in piece_refs], axis=0
    )


def both_kernel(x_ref, y_ref, out_ref):
    rows = x_ref.shape[0]
    out_ref[pl.ds(0, rows), :] = x_ref[...]
    out_ref[pl.ds(rows, rows), :] = y_ref[...]


def stack_kernel(rows, own, near_a, near_b, far_a, far_b, other, mid_ref, right_ref):
    for half in range(2):
        place = pl.ds(half * rows, rows)
        beside = pl.ds((2 + half) * rows, rows)
        blocks = (own[place, :], near_a[place, :] + far_a[place, :], near_b[place, :] + far_b[place, :])
        others = (other[place, :], far_a[beside, :], far_b[beside, :])
        for i in range(3):
            mid_ref[pl.ds((3 * half + i) * rows, rows), :] = blocks[i]
            right_ref[pl.ds((3 * half + i) * rows, rows), :] = others[i]


def join_kernel(x_ref, y_ref, out_ref):
    out_ref[...] = x_ref[...] + y_ref[...]


def scores_kernel(position, *refs):
    bias_ref, *refs = refs
    *pieces, kv_ref, weights_ref, stats_ref = refs
    if position == 0:
        saved_ref, *pieces = pieces
    heads = pieces[0].shape[1] // HEAD_DIM
    rows = pieces[0].shape[0] // 2
    stats_ref[...] = jnp.zeros_like(stats_ref)
    for head in range(heads):
        cols = head_cols(head)
        query = gathered(pieces, 0, head)
        if position == 0:
            product = pieces[0][pl.ds(rows, rows), cols].astype(F32)
            product = product * saved_ref[:, cols].astype(F32)
            ones = jnp.ones((8, HEAD_DIM), F32)
            row_dot = dot(ones, product, NT, lax.Precision.HIGHEST)[:1]
            stats_ref[2 * heads + head : 2 * heads + head + 1, 0:rows] = row_dot
        scores = []
        tops = []
        for row in range(3):
            key = kv_ref[pl.ds(row * rows, rows), cols]
            at = 3 * position + row
            s = dot(key, query, NT)
            scores.append(s)
            tops.append(jnp.max(s, axis=0, keepdims=True) * SCALE2 - bias_ref[at : at + 1, :])
        top = jnp.maximum(functools.reduce(jnp.maximum, tops), -0.5 * CLOSED)
        total = jnp.zeros_like(top)
        for row, s in enumerate(scores):
            at = 3 * position + row
            raised = jnp.exp2(s * SCALE2 - (top + bias_ref[at : at + 1, :]))
            weights_ref[head, pl.ds(row * rows, rows), :] = raised
            total = total + jnp.sum(raised, axis=0, keepdims=True)
        stats_ref[head : head + 1, :] = top
        stats_ref[heads + head : heads + head + 1, :] = total


def table_kernel(heads, *refs):
    *stats, out_ref = refs
    out_ref[...] = stats[0][...]
    top = functools.reduce(jnp.maximum, [ref[0:heads, :] for ref in stats])
    total = sum(ref[heads : 2 * heads, :] * jnp.exp2(ref[0:heads, :] - top) for ref in stats)
    out_ref[0:heads, :] = top
    out_ref[heads : 2 * heads, :] = total


def reordered(table, rows, flip):
    if flip == 0:
        return table
    return jnp.concatenate(
        [table[:, (j ^ flip) * rows : ((j ^ flip) + 1) * rows] for j in range(4)], axis=1
    )


def merge_kernel(heads, rows, *refs):
    *tables, out_ref = refs
    tables = [reordered(ref[...], rows, flip) for flip, ref in zip((1, 3, 2, 0), tables)]
    out_ref[...] = jnp.zeros_like(out_ref)
    top = functools.reduce(jnp.maximum, [t[0:heads] for t in tables])
    total = sum(t[heads : 2 * heads] * jnp.exp2(t[0:heads] - top) for t in tables)
    out_ref[0:heads, :] = top + jnp.log2(total)
    out_ref[heads : 2 * heads, :] = sum(t[2 * heads : 3 * heads] for t in tables)


def product_kernel(*refs):
    *pieces, kv_ref, out_ref = refs
    rows = pieces[0].shape[0] // 2
    for head in range(pieces[0].shape[1] // HEAD_DIM):
        cols = head_cols(head)
        grad = gathered(pieces, 1, head)
        for row in range(3):
            value = kv_ref[pl.ds((3 + row) * rows, rows), cols]
            out_ref[head, pl.ds(row * rows, rows), :] = dot(value, grad, NT)


def grads_kernel(stage, *refs):
    lse_ref, stats_ref, weights_ref, p0, p1, p2, p3, product_ref, kv_ref, *refs = refs
    pieces = (p0, p1, p2, p3)
    if stage == 0:
        out_ref, kept_ref = refs
    elif stage == 1:
        kept_ref, kept_kv_ref, out_ref, dq_ref = refs
    else:
        prior_ref, out_ref, dq_ref = refs
    heads = p0.shape[1] // HEAD_DIM
    rows = p0.shape[0] // 2
    for head in range(heads):
        cols = head_cols(head)
        query = gathered(pieces, 0, head)
        grad = gathered(pieces, 1, head)
        scale = jnp.exp2(stats_ref[head : head + 1, :] - lse_ref[head : head + 1, :])
        row_dot = lse_ref[heads + head : heads + head + 1, :] * SCALE
        if stage == 1:
            whole = pl.ds(0, 3 * rows)
            dq = dot(kept_ref[head], kept_kv_ref[whole, cols], TN)
        elif stage == 2:
            dq = prior_ref[:, cols]
        for row in range(3):
            place = pl.ds(row * rows, rows)
            weights = weights_ref[head, place, :] * scale
            score_grad = weights * (product_ref[head, place, :] * SCALE - row_dot)
            score_grad = score_grad.astype(BF16)
            out_ref[place, cols] = dot(score_grad, query, NN).astype(out_ref.dtype)
            value_part = dot(weights.astype(BF16), grad, NN).astype(out_ref.dtype)
            out_ref[pl.ds((3 + row) * rows, rows), cols] = value_part
            if stage == 0:
                kept_ref[head, place, :] = score_grad
            else:
                dq = dq + dot(score_grad, kv_ref[place, cols], TN)
        if stage:
            dq_ref[:, cols] = dq


def add_kernel(x_ref, y_ref, out_ref):
    out_ref[...] = x_ref[...] + y_ref[...].astype(F32)


def column_kernel(rows, mid_ref, a_ref, own_ref, to_a_ref, to_b_ref):
    for half in range(2):
        for row, out in enumerate((own_ref, to_a_ref, to_b_ref)):
            place = pl.ds((3 * half + row) * rows, rows)
            total = mid_ref[place, :] + a_ref[place, :].astype(F32)
            out[pl.ds(half * rows, rows), :] = total.astype(out.dtype)


def query_kernel(own_ref, a_ref, b_ref, c_ref, out_ref):
    total = own_ref[...] + a_ref[...].astype(F32) + b_ref[...].astype(F32)
    out_ref[...] = (total + c_ref[...].astype(F32)).astype(BF16)


def finish_kernel(dq_ref, own_ref, a_ref, b_ref, query_ref, key_ref, value_ref):
    rows = dq_ref.shape[0]
    query_ref[...] = dq_ref[...]
    for half, out in enumerate((key_ref, value_ref)):
        place = pl.ds(half * rows, rows)
        total = own_ref[place, :] + a_ref[place, :].astype(F32) + b_ref[place, :].astype(F32)
        out[...] = total.astype(BF16)


def call(kernel, out_shape, *args):
    many = isinstance(out_shape, (tuple, list))
    vmem = pl.BlockSpec(memory_space=pltpu.VMEM)
    return pl.pallas_call(
        kernel,
        out_shape=out_shape,
        in_specs=[vmem] * len(args),
        out_specs=[vmem] * len(out_shape) if many else vmem,
        compiler_params=pltpu.CompilerParams(vmem_limit_bytes=16 * 1024 * 1024),
        name=getattr(kernel, "func", kernel).__name__[:-7],
        cost_estimate=pl.CostEstimate(flops=0, bytes_accessed=0, transcendentals=0),
    )(*args)


def after(x, *others):
    return lax.optimization_barrier((x, *others))[0]


def local(query_in, key_in, value_in, saved_out, out_grad, window_mask):
    frames_dev, _, tile_rows, tile_cols, width = query_in.shape
    rows = frames_dev * tile_rows * tile_cols
    heads = width // HEAD_DIM
    n_ta = lax.axis_size("ta")
    row_tiles, col_tiles = window_mask.shape[1:3]
    me = lax.axis_index("ta")
    plane = lax.axis_index("ha")
    row_tile = plane // col_tiles
    col_tile = plane % col_tiles

    def pairs(count, first):
        ends = [(i, i + 1) for i in range(first, count - 1, 2)]
        return ends + [(d, s) for s, d in ends]

    far = (col_tiles // 2 - 1, col_tiles // 2)
    near = [c for c in range(col_tiles) if c not in far]

    def row_swap(x, first, columns, name):
        route = [
            (s * col_tiles + c, d * col_tiles + c)
            for s, d in pairs(row_tiles, first)
            for c in columns
        ]
        with jax.named_scope(name):
            return lax.ppermute(x, "ha", route)

    def col_swap(x, ends, name):
        route = [(r * col_tiles + s, r * col_tiles + d) for s, d in ends for r in range(row_tiles)]
        with jax.named_scope(name):
            return lax.ppermute(x, "ha", route)

    inner = pairs(col_tiles, 0)
    outer = pairs(col_tiles, 1)
    middle = [pair for pair in outer if pair[0] in far]
    outside = [pair for pair in outer if pair[0] not in far]

    def ta_swap(x, flip, name):
        with jax.named_scope(name):
            return lax.ppermute(x, "ta", [(i, i ^ flip) for i in range(n_ta)])

    q, k, v, o, g = (
        x.reshape(rows, width) for x in (query_in, key_in, value_in, saved_out, out_grad)
    )
    kv = jnp.concatenate([k, v], axis=0)
    kv_far = col_swap(kv, middle, "kv_far")
    kv_b = row_swap(kv, 1, near, "kv_row_1")
    kv_a = row_swap(kv, 0, near, "kv_row_0")
    qg = jnp.concatenate([q, g], axis=0)
    swapped = {flip: ta_swap(qg, flip, "query_ta") for flip in (2, 1, 3)}
    pieces = [qg] + [swapped[flip] for flip in (1, 2, 3)]
    two_shape = jax.ShapeDtypeStruct((4 * rows, width), BF16)
    stack_shape = jax.ShapeDtypeStruct((6 * rows, width), BF16)
    both = call(both_kernel, two_shape, kv, kv_far)
    both_b = row_swap(both, 1, far, "far_row_1")
    both_a = row_swap(both, 0, far, "far_row_0")
    kv_mid, kv_right = call(
        functools.partial(stack_kernel, rows), (stack_shape, stack_shape),
        kv, kv_a, kv_b, both_a, both_b, kv_far,
    )
    kv_out = col_swap(kv_mid, outside, "kv_col_1")
    kv_left = col_swap(kv_mid, inner, "kv_col_0")
    kv_right = call(join_kernel, stack_shape, kv_right, kv_out)

    place = jnp.arange(16, dtype=jnp.int32)
    row_step = jnp.where(place < 9, place % 3, 0)
    row_step = jnp.where(row_step == 2, -1, row_step) * (1 - 2 * (row_tile % 2))
    col_step = jnp.where(place < 9, place // 3, 0)
    col_step = jnp.where(col_step == 2, -1, col_step) * (1 - 2 * (col_tile % 2))
    inside = (row_tile + row_step >= 0) & (row_tile + row_step < row_tiles)
    inside = inside & (col_tile + col_step >= 0) & (col_tile + col_step < col_tiles) & (place < 9)
    key_time = me * frames_dev // TILE_T
    owner = me ^ jnp.arange(n_ta, dtype=jnp.int32)
    query_time = owner * frames_dev // TILE_T
    windows = lax.dynamic_slice(
        window_mask, (0, row_tile, col_tile, 0), (window_mask.shape[0], 1, 1, 27)
    ).reshape(-1, 27)
    code = (key_time - query_time[None, :] + 1) * 9 + ((row_step + 1) * 3 + col_step + 1)[:, None]
    number = jnp.arange(27, dtype=jnp.int32)
    hit = code[:, :, None] == number
    table = jnp.zeros((16, n_ta), jnp.int32)
    for t in range(window_mask.shape[0]):
        found = jnp.sum(jnp.where(hit, windows[t], 0), axis=-1)
        table = jnp.where(query_time[None, :] == t, found, table)
    bias = jnp.where((table == 1) & inside[:, None], 0.0, CLOSED).astype(F32)
    bias = jnp.repeat(bias, rows, axis=1)

    n_q = n_ta * rows
    stat_shape = jax.ShapeDtypeStruct((8, n_q), F32)
    weight_shape = jax.ShapeDtypeStruct((heads, 3 * rows, n_q), F32)
    dq_shape = jax.ShapeDtypeStruct((n_q, width), F32)

    def scores(position, kv):
        kernel = functools.partial(scores_kernel, position)
        first = (o,) if position == 0 else ()
        return call(kernel, (weight_shape, stat_shape), bias, *first, *pieces, kv)

    def products(kv):
        return call(product_kernel, weight_shape, *pieces, kv)

    w_mid, s_mid = scores(0, kv_mid)
    w_a, s_a = scores(1, kv_left)
    w_b, s_b = scores(2, kv_right)
    mine = call(functools.partial(table_kernel, heads), stat_shape, s_mid, s_a, s_b)
    swapped = {flip: ta_swap(mine, flip, "stats_ta") for flip in (2, 1, 3)}
    others = tuple(swapped[flip] for flip in (1, 3, 2))
    p_mid, p_a, p_b = products(kv_mid), products(kv_left), products(kv_right)
    others = after(others, p_a, p_b, p_mid)
    lse = call(functools.partial(merge_kernel, heads, rows), stat_shape, *others, mine)

    def grads(stage, stats, weights, product, kv, dtype, *prior):
        part = jax.ShapeDtypeStruct((6 * rows, width), dtype)
        kept = jax.ShapeDtypeStruct(weight_shape.shape, BF16)
        return call(
            functools.partial(grads_kernel, stage),
            (part, dq_shape if stage else kept),
            lse, stats, weights, *pieces, product, kv, *prior,
        )

    d_b, kept = grads(0, s_b, w_b, p_b, kv_right, BF16)
    d_b = col_swap(d_b, outer, "d_col_1")
    d_a, dq = grads(1, s_a, w_a, p_a, kv_left, BF16, kept, kv_right)
    d_a = col_swap(d_a, inner, "d_col_0")
    d_mid, dq = grads(2, s_mid, w_mid, p_mid, kv_mid, F32, dq)
    dq = dq.reshape(n_ta, rows, width)
    dq_parts = [ta_swap(dq[flip], flip, "dq_ta") for flip in (1, 3, 2)]
    d_mid = call(add_kernel, jax.ShapeDtypeStruct(d_mid.shape, F32), d_mid, d_b)
    own = jax.ShapeDtypeStruct((2 * rows, width), F32)
    sent = jax.ShapeDtypeStruct((2 * rows, width), BF16)
    own, to_a, to_b = call(
        functools.partial(column_kernel, rows), (own, sent, sent), d_mid, d_a
    )
    d_b = row_swap(to_b, 1, range(col_tiles), "d_row_1")
    d_a = row_swap(to_a, 0, range(col_tiles), "d_row_0")
    one = jax.ShapeDtypeStruct((rows, width), BF16)
    dq = call(query_kernel, one, dq[0], *dq_parts)
    outs = call(finish_kernel, (one, one, one), dq, own, d_a, d_b)
    return tuple(x.reshape(query_in.shape) for x in outs)


def solution(mesh):
    spec = P("ta", "ha", None, None, "ga")
    return jax.shard_map(
        local,
        mesh=mesh,
        in_specs=(spec,) * 5 + (P(),),
        out_specs=(spec,) * 3,
        check_vma=False,
    )
```
